256 devices in a mesh: seq: 32 (over z, x_lo, core), head: 8 (over x_hi, y).
Axes of the slice: x: 4 (x_hi: 2, x_lo: 2; x = x_hi * 2 + x_lo), y: 4, z: 8, core: 2. Of those that a mesh axis runs over, the one named last changes fastest.
Arguments:
- q_raw: bfloat16 [32768, 4096], P('seq', 'head'), may hold values from -6 to 6
- k_raw: bfloat16 [32768, 2048], P('seq', 'head'), may hold values from -6 to 6
- values: bfloat16 [32768, 2048], P('seq', 'head'), may hold values from -6 to 6
- grad_out: bfloat16 [32768, 4096], P('seq', 'head'), may hold values from -6 to 6
- segment_ids: int32 [32768], replicated, may hold values from 0 to 31, never falling along the last dimension, each value on 1 to 2048 neighbouring positions
- q_gain: float32 [128], replicated, may hold values from 0.5 to 4
- k_gain: float32 [128], replicated, may hold values from 0.5 to 4
Outputs:
- q_grad: bfloat16 [32768, 4096], P('seq', 'head')
- k_grad: bfloat16 [32768, 2048], P('seq', 'head')
- v_grad: bfloat16 [32768, 2048], P('seq', 'head')
- q_gain_grad: float32 [128], replicated
- k_gain_grad: float32 [128], replicated
The draws below stay inside these ranges and needn't reach their ends.
Inputs may be any that keep to these rules, and one draw needn't show every extreme that they name: `segment_ids`: ids never fall along the tokens; some document holds exactly 2048 tokens.
All inputs are finite; a program needn't handle non-finite values.
Results may differ from the reference program's by a relative error of at most 0.033.
The reference program's roundings to bfloat16 on the way count: a program that leaves them out, or rounds other values in their place, can miss the bound.
Values may be sent and summed in bfloat16 or wider, within the bound.
No kernel may reach another device: no remote copies, remote signals or barrier semaphores. Data moves between devices by JAX's collectives and lax.ppermute only.
A program may use at most 128 MiB of HBM per device.

```python
import math
import jax
import jax.numpy as jnp
import numpy as np
from jax import lax

QHEADS = 32
KVHEADS = 16
HEAD_DIM = 128
WINDOW = 1024
TOK_DEV = 1024
BLOCK = 512
TOKENS = 32768


def key_field(key):
    return jax.random.normal(jax.random.fold_in(key, 11), (TOKENS, KVHEADS, HEAD_DIM), jnp.float32)


def draw_k_raw(key, part):
    field = jnp.clip(key_field(key), -6.0, 6.0)
    return field.reshape(TOKENS, KVHEADS * HEAD_DIM).astype(jnp.bfloat16)


def draw_q_raw(key, part):
    fresh = jax.random.normal(jax.random.fold_in(key, 21), (TOKENS, QHEADS, HEAD_DIM), jnp.float32)
    fresh = jnp.clip(fresh, -6.0, 6.0)
    return fresh.reshape(TOKENS, QHEADS * HEAD_DIM).astype(jnp.bfloat16)


def draw_q_gain(key, part):
    return jax.random.uniform(jax.random.fold_in(key, 32), (HEAD_DIM,), jnp.float32, 0.5, 2.0)


def draw_k_gain(key, part):
    return jax.random.uniform(jax.random.fold_in(key, 42), (HEAD_DIM,), jnp.float32, 0.5, 2.0)


def block_scale(stream_key, extent, split, least, top_value):
    level, own = 1.0, jax.random.fold_in(stream_key, 6)
    for position, blocks in split:
        steps = jnp.exp(jax.random.uniform(jax.random.fold_in(own, position), (blocks,), jnp.float32, least / len(split), top_value / len(split)))
        level = level * jnp.repeat(steps, extent[position] // blocks).reshape([-1 if axis == position else 1 for axis in range(len(extent))])
    return level


def profile(count, total, most, slope):
    loads = [(1 << 20) // math.isqrt(grade ** slope) + 1 for grade in range(2, count + 1)]
    rest, counts = total - most - (count - 1), [1] * (count - 1)
    while rest > 0:
        candidates = [i for i in range(count - 1) if counts[i] < most]
        mass, left = sum([loads[i] for i in candidates]), rest
        for i in candidates:
            addition = min(most - counts[i], max(1, left * loads[i] // mass), rest)
            counts[i] = counts[i] + addition
            rest = rest - addition
    return np.array([most] + counts)


def ragged(stream_key, number_of, total, most, lean):
    if number_of == 2:
        one = jax.random.randint(stream_key, (), max(1, total - most), min(most, total - 1) + 1)
        return jnp.stack([one, total - one])
    tallies = jnp.asarray(profile(number_of, total, most, lean), jnp.int32)
    pairs = (number_of - 1) // 2
    source_of, sink = tallies[1:1 + 2 * pairs:2], tallies[2:2 + 2 * pairs:2]
    room = jnp.minimum(source_of - 1, most - sink)
    passed = jax.random.randint(jax.random.fold_in(stream_key, 1), (pairs,), 0, 1 << 20) % (room + 1)
    tallies = tallies.at[1:1 + 2 * pairs:2].set(source_of - passed).at[2:2 + 2 * pairs:2].set(sink + passed)
    return tallies[jax.random.permutation(jax.random.fold_in(stream_key, 2), number_of)]


def centred(rng, shape, deviation, limit, cuts=(), kind=jnp.bfloat16):
    drawn = deviation * jax.random.normal(rng, shape, jnp.float32)
    if cuts:
        drawn = drawn * block_scale(rng, shape, cuts, -0.22, 0.18)
    return jnp.clip(drawn, -limit, limit).astype(kind)


def setup_inputs(seed: int = 0) -> dict:
    arg_keys = jax.random.split(jax.random.key(seed), 8)
    q_raw = draw_q_raw(jax.random.fold_in(arg_keys[7], 71), 0)
    k_raw = draw_k_raw(jax.random.fold_in(arg_keys[7], 71), 0)
    values = centred(arg_keys[2], (TOKENS, KVHEADS * HEAD_DIM), 1.0, 6.0, ((0, 32), (1, 8)))
    grad_out = centred(arg_keys[3], (TOKENS, QHEADS * HEAD_DIM), 1.0, 6.0, ((0, 32), (1, 8)))
    segment_ids = jnp.searchsorted(jnp.cumsum(ragged(arg_keys[4], TOKENS // TOK_DEV, TOKENS, 2 * TOK_DEV, 2)), jnp.arange(TOKENS), side="right").astype(jnp.int32)
    q_gain = draw_q_gain(jax.random.fold_in(arg_keys[7], 71), 0)
    k_gain = draw_k_gain(jax.random.fold_in(arg_keys[7], 71), 0)
    return dict(q_raw=q_raw, k_raw=k_raw, values=values, grad_out=grad_out, segment_ids=segment_ids, q_gain=q_gain, k_gain=k_gain)


SCALE = 168.0 ** (-0.5)
EPS = 1e-06
BASE = 10000.0

def angles(positions, dim):
    half = dim // 2
    freq = BASE ** (-jnp.arange(half, dtype=jnp.float32) * 2.0 / dim)
    angle = positions.astype(jnp.float32)[:, None] * freq[None, :]
    angle = jnp.concatenate([angle, angle], axis=1)
    return (jnp.cos(angle), jnp.sin(angle))

def rotate(x):
    half = x.shape[-1] // 2
    return jnp.concatenate([-x[..., half:], x[..., :half]], axis=-1)

def rotate_back(z):
    half = z.shape[-1] // 2
    return jnp.concatenate([z[..., half:], -z[..., :half]], axis=-1)

def normed(raw, gain, cosv, sinv, factor):
    x = raw.astype(jnp.float32)
    rstd = lax.rsqrt(lax.optimization_barrier(jnp.mean(x * x, axis=-1, keepdims=True)) + EPS)
    y = x * rstd * gain
    out = (y * cosv[:, None, :] + rotate(y) * sinv[:, None, :]) * factor
    return (out.astype(jnp.bfloat16), rstd)

def norm_back(raw, gain, rstd, grad, cosv, sinv, factor):
    x = raw.astype(jnp.float32)
    g = grad * factor
    dy = g * cosv[:, None, :] + rotate_back(g * sinv[:, None, :])
    gy = dy * gain
    dx = rstd * gy - x * rstd * rstd * rstd * lax.optimization_barrier(jnp.mean(gy * x, axis=-1, keepdims=True))
    return (dx.astype(jnp.bfloat16), lax.optimization_barrier(jnp.sum(dy * x * rstd, axis=(0, 1))))

def allowed(qpos, kpos, qseg, kseg):
    gap = qpos[:, None] - kpos[None, :]
    return (qseg[:, None] == kseg[None, :]) & (gap >= 0) & (gap < WINDOW)

def attend(qb, kb, vb, gb, mask):
    f32 = jnp.float32
    qf, kf, vf, gf = (qb.astype(f32), kb.astype(f32), vb.astype(f32), gb.astype(f32))
    scores = jnp.einsum('qhgd,khd->hgqk', qf, kf, preferred_element_type=f32)
    masked = jnp.where(mask, scores, -jnp.inf)
    top = lax.optimization_barrier(jnp.max(masked, axis=-1, keepdims=True))
    lse = top + jnp.log(lax.optimization_barrier(jnp.sum(jnp.exp(masked - top), axis=-1, keepdims=True)))
    prob = jnp.where(mask, jnp.exp(scores - lse), 0.0)
    weights = prob.astype(jnp.bfloat16).astype(f32)
    output = jnp.einsum('hgqk,khd->qhgd', weights, vf, preferred_element_type=f32)
    delta = jnp.transpose(lax.optimization_barrier(jnp.sum(gf * output, axis=-1)), (1, 2, 0))
    dprob = jnp.einsum('qhgd,khd->hgqk', gf, vf, preferred_element_type=f32)
    dscore = (prob * (dprob - delta[..., None])).astype(jnp.bfloat16).astype(f32)
    dq = jnp.einsum('hgqk,khd->qhgd', dscore, kf, preferred_element_type=f32)
    dk = jnp.einsum('hgqk,qhgd->khd', dscore, qf, preferred_element_type=f32)
    dv = jnp.einsum('hgqk,qhgd->khd', weights, gf, preferred_element_type=f32)
    return (dq, dk, dv)

def reference(q_raw, k_raw, values, grad_out, segment_ids, q_gain, k_gain):
    tokens = q_raw.shape[0]
    dim = HEAD_DIM
    group = QHEADS // KVHEADS
    positions = jnp.arange(tokens, dtype=jnp.int32)
    cosv, sinv = angles(positions, dim)
    queries, q_rstd = normed(q_raw.reshape(tokens, QHEADS, dim), q_gain, cosv, sinv, SCALE)
    keys, k_rstd = normed(k_raw.reshape(tokens, KVHEADS, dim), k_gain, cosv, sinv, 1.0)
    vals = values.reshape(tokens, KVHEADS, dim)
    grads = grad_out.reshape(tokens, KVHEADS, group, dim)
    qgroups = queries.reshape(tokens, KVHEADS, group, dim)
    all_keys = jnp.concatenate([jnp.zeros((WINDOW, KVHEADS, dim), jnp.bfloat16), keys], axis=0)
    all_vals = jnp.concatenate([jnp.zeros((WINDOW, KVHEADS, dim), jnp.bfloat16), vals], axis=0)
    k_pos = jnp.arange(tokens + WINDOW, dtype=jnp.int32) - WINDOW
    k_seg = jnp.concatenate([jnp.full((WINDOW,), -1, jnp.int32), segment_ids])
    span = WINDOW + BLOCK

    def step(carry, index):
        dk_acc, dv_acc = carry
        first = (index * BLOCK).astype(jnp.int32)
        qb = lax.dynamic_slice_in_dim(qgroups, first, BLOCK)
        gb = lax.dynamic_slice_in_dim(grads, first, BLOCK)
        kb = lax.dynamic_slice_in_dim(all_keys, first, span)
        vb = lax.dynamic_slice_in_dim(all_vals, first, span)
        mask = allowed(lax.dynamic_slice_in_dim(positions, first, BLOCK), lax.dynamic_slice_in_dim(k_pos, first, span), lax.dynamic_slice_in_dim(segment_ids, first, BLOCK), lax.dynamic_slice_in_dim(k_seg, first, span))
        dq, dk, dv = attend(qb, kb, vb, gb, mask)
        dk_acc = lax.dynamic_update_slice_in_dim(dk_acc, lax.dynamic_slice_in_dim(dk_acc, first, span) + dk, first, 0)
        dv_acc = lax.dynamic_update_slice_in_dim(dv_acc, lax.dynamic_slice_in_dim(dv_acc, first, span) + dv, first, 0)
        return ((dk_acc, dv_acc), dq)
    zeros = jnp.zeros((tokens + WINDOW, KVHEADS, dim), jnp.float32)
    (dk_acc, dv_acc), dq_blocks = lax.scan(step, (zeros, zeros), jnp.arange(tokens // BLOCK, dtype=jnp.int32))
    dq_all = dq_blocks.reshape(tokens, QHEADS, dim)
    q_grad, q_gain_grad = norm_back(q_raw.reshape(tokens, QHEADS, dim), q_gain, q_rstd, dq_all, cosv, sinv, SCALE)
    k_grad, k_gain_grad = norm_back(k_raw.reshape(tokens, KVHEADS, dim), k_gain, k_rstd, dk_acc[WINDOW:], cosv, sinv, 1.0)
    v_grad = dv_acc[WINDOW:].astype(jnp.bfloat16)
    return (q_grad.reshape(tokens, QHEADS * dim), k_grad.reshape(tokens, KVHEADS * dim), v_grad.reshape(tokens, KVHEADS * dim), q_gain_grad, k_gain_grad)
```

```python
import functools

import jax
import jax.numpy as jnp
import numpy as np
from jax import lax
from jax.experimental import pallas as pl
from jax.experimental.pallas import tpu as pltpu
from jax.sharding import PartitionSpec as P

WINDOW = 1024
BLOCK = 256
SCALE = 168.0 ** (-0.5)
EPS = 1e-06
BASE = 10000.0
LOG2E = 1.4426950408889634
LN2 = 0.6931471805599453
NEG = -1e30
APART = -32768.0
NO_DOC = 64
F32 = jnp.float32
BF16 = jnp.bfloat16
NT = (((1,), (1,)), ((), ()))
NN = (((1,), (0,)), ((), ()))
TN = (((0,), (0,)), ((), ()))


def shifted(block, axis, distance):
    devices = range(lax.axis_size(axis))
    route = [(i - distance, i) for i in devices if i - distance in devices]
    return lax.ppermute(block, axis, route)


def tables(tok, devices, dim):
    half = dim // 2
    freq = BASE ** (-np.arange(half, dtype=np.float64) * 2.0 / dim)
    freq = np.concatenate([freq, freq])
    sign = np.concatenate([-np.ones(half), np.ones(half)])
    inner = np.arange(tok, dtype=np.float64)[:, None] * freq
    rows = -(-(devices + 1) // 8) * 8
    outer = (np.arange(rows, dtype=np.float64)[:, None] - 1.0) * tok * freq
    return tuple(
        np.asarray(a, np.float32)
        for a in (np.cos(inner), np.sin(inner) * sign, np.cos(outer), np.sin(outer) * sign)
    )


def dot(a, b, dims):
    return lax.dot_general(a, b, dims, preferred_element_type=F32)


def turn(cos_ref, sin_ref, cdev_ref, sdev_ref, row):
    cl, sl = cos_ref[...], sin_ref[...]
    cd, sd = cdev_ref[pl.ds(row, 1), :], sdev_ref[pl.ds(row, 1), :]
    return cl * cd - sl * sd, sl * cd + cl * sd


def swap(y):
    return pltpu.roll(y, y.shape[-1] // 2, 1)


def inverse_rms(x):
    return lax.rsqrt(jnp.mean(x * x, axis=-1, keepdims=True) + EPS)


def normed(raw, gain, cosv, sinv):
    x = raw.astype(F32)
    y = x * inverse_rms(x) * gain
    return (y * cosv + swap(y) * sinv).astype(BF16)


def unturn(g, cosv, sinv):
    return g * cosv - swap(g) * sinv


def doc_rows(seg):
    row = jnp.concatenate([seg[i : i + 1, :] for i in range(seg.shape[0])], axis=1)
    ids = lax.broadcasted_iota(jnp.int32, (128, row.shape[1]), 0)
    return jnp.where(ids == row, 1.0, 0.0).T


def query_side(onehot):
    return ((1.0 - onehot) * APART).astype(BF16)


def corner(strict):
    k = lax.broadcasted_iota(jnp.int32, (BLOCK, BLOCK), 0)
    q = lax.broadcasted_iota(jnp.int32, (BLOCK, BLOCK), 1)
    return k > q if strict else k <= q


def masked_tail(score, inside):
    edge = score.shape[0] - BLOCK
    if edge == 0:
        return jnp.where(inside, score, NEG)
    return jnp.concatenate([score[:edge], jnp.where(inside, score[edge:], NEG)], axis=0)


def masked_head(score, inside):
    if score.shape[0] == BLOCK:
        return jnp.where(inside, score, NEG)
    return jnp.concatenate([jnp.where(inside, score[:BLOCK], NEG), score[BLOCK:]], axis=0)


def stats_kernel(
    q_ref, k_ref, v_ref, g_ref, seg_ref, qgain_ref, kgain_ref, cos_ref, sin_ref, cdev_ref, sdev_ref,
    qh_ref, kh_ref, stat_ref,
):
    tok, dim = k_ref.shape
    group = q_ref.shape[1] // dim
    s = lax.axis_index("seq")
    cosv, sinv = turn(cos_ref, sin_ref, cdev_ref, sdev_ref, s + 1)
    onehot = doc_rows(seg_ref[pl.ds(s, 1)][0])
    kh = normed(k_ref[...], kgain_ref[...], cosv, sinv)
    kh_ref[...] = kh
    kside = jnp.concatenate([kh, onehot.astype(BF16)], axis=1)
    qdoc = query_side(onehot)
    inside = corner(False)
    for g in range(group):
        cols = slice(g * dim, (g + 1) * dim)
        qh = normed(q_ref[:, cols], qgain_ref[...] * (SCALE * LOG2E), cosv, sinv)
        qh_ref[:, cols] = qh
        qside = jnp.concatenate([qh, qdoc], axis=1)
        for i in range(tok // BLOCK):
            rows = slice(i * BLOCK, (i + 1) * BLOCK)
            top = (i + 1) * BLOCK
            score = dot(kside[:top], qside[rows], NT)
            score = masked_tail(score, inside)
            dprob = dot(v_ref[:top, :], g_ref[rows, cols], NT)
            m = jnp.max(score, axis=0, keepdims=True)
            e = jnp.exp2(score - m)
            stat_ref[0, g : g + 1, rows] = m
            stat_ref[0, group + g : group + g + 1, rows] = jnp.sum(e, axis=0, keepdims=True)
            stat_ref[0, 2 * group + g : 2 * group + g + 1, rows] = jnp.sum(e * dprob, axis=0, keepdims=True)


def halo_kernel(
    qh_ref, k_ref, v_ref, g_ref, seg_ref, kgain_ref, cos_ref, sin_ref, cdev_ref, sdev_ref, stat_ref,
    dq_ref, dk_ref, dv_ref, fin_ref, part_ref, ds_ref, pb_ref,
):
    tok, dim = k_ref.shape
    group = qh_ref.shape[1] // dim
    s = lax.axis_index("seq")
    cosv, sinv = turn(cos_ref, sin_ref, cdev_ref, sdev_ref, s)
    qdoc = query_side(doc_rows(seg_ref[pl.ds(s, 1)][0]))
    before = seg_ref[pl.ds(jnp.maximum(s - 1, 0), 1)][0]
    kdoc = doc_rows(jnp.where(s == 0, NO_DOC, before)).astype(BF16)
    kh = normed(k_ref[...], kgain_ref[...], cosv, sinv)
    kside = jnp.concatenate([kh, kdoc], axis=1)
    inside = corner(True)
    for g in range(group):
        cols = slice(g * dim, (g + 1) * dim)
        qside = jnp.concatenate([qh_ref[:, cols], qdoc], axis=1)
        for i in range(tok // BLOCK):
            rows = slice(i * BLOCK, (i + 1) * BLOCK)
            low = i * BLOCK
            score = dot(kside[low:], qside[rows], NT)
            score = masked_head(score, inside)
            dprob = dot(v_ref[low:, :], g_ref[rows, cols], NT)
            m_own = stat_ref[0, g : g + 1, rows]
            m = jnp.maximum(m_own, jnp.max(score, axis=0, keepdims=True))
            e = jnp.exp2(score - m)
            keep = jnp.exp2(m_own - m)
            total = stat_ref[0, group + g : group + g + 1, rows] * keep + jnp.sum(e, axis=0, keepdims=True)
            moment = stat_ref[0, 2 * group + g : 2 * group + g + 1, rows] * keep + jnp.sum(
                e * dprob, axis=0, keepdims=True
            )
            inv = 1.0 / total
            delta = moment * inv
            fin_ref[0, g : g + 1, rows] = m + jnp.log2(total)
            fin_ref[0, group + g : group + g + 1, rows] = delta
            p = e * inv
            ds = (p * (dprob - delta)).astype(BF16)
            spot = slice(g * tok + i * BLOCK, g * tok + (i + 1) * BLOCK)
            pb_ref[low:, spot] = p.astype(BF16)
            ds_ref[low:, spot] = ds
            dq_ref[rows, cols] = dot(ds, kh[low:], TN)
    part = jnp.zeros((8, dim), F32)
    for j in range(tok // BLOCK):
        rows = slice(j * BLOCK, (j + 1) * BLOCK)
        high = (j + 1) * BLOCK
        dk, dv = 0.0, 0.0
        for g in range(group):
            spot = slice(g * tok, g * tok + high)
            cols = slice(g * dim, (g + 1) * dim)
            dk = dk + dot(ds_ref[rows, spot], qh_ref[:high, cols], NN)
            dv = dv + dot(pb_ref[rows, spot], g_ref[:high, cols], NN)
        dy = unturn(dk * LN2, cosv[rows], sinv[rows])
        x = k_ref[rows, :].astype(F32)
        part = part + jnp.sum((dy * x * inverse_rms(x)).reshape(BLOCK // 8, 8, dim), axis=0)
        dk_ref[rows, :] = dy.astype(BF16)
        dv_ref[rows, :] = dv.astype(BF16)
    part_ref[0] = part


def own_kernel(
    qh_ref, kh_ref, v_ref, g_ref, q_ref, k_ref, seg_ref, qgain_ref, cos_ref, sin_ref, cdev_ref, sdev_ref,
    fin_ref, dqp_ref, qg_ref, dy_ref, dv_ref, part_ref, ds_ref, pb_ref,
):
    tok, dim = kh_ref.shape
    group = qh_ref.shape[1] // dim
    s = lax.axis_index("seq")
    cosv, sinv = turn(cos_ref, sin_ref, cdev_ref, sdev_ref, s + 1)
    onehot = doc_rows(seg_ref[pl.ds(s, 1)][0])
    kh = kh_ref[...]
    kside = jnp.concatenate([kh, onehot.astype(BF16)], axis=1)
    qdoc = query_side(onehot)
    inside = corner(False)
    gain = qgain_ref[...]
    qpart = jnp.zeros((8, dim), F32)
    for g in range(group):
        cols = slice(g * dim, (g + 1) * dim)
        qside = jnp.concatenate([qh_ref[:, cols], qdoc], axis=1)
        for i in range(tok // BLOCK):
            rows = slice(i * BLOCK, (i + 1) * BLOCK)
            top = (i + 1) * BLOCK
            score = dot(kside[:top], qside[rows], NT)
            score = masked_tail(score, inside)
            dprob = dot(v_ref[:top, :], g_ref[rows, cols], NT)
            p = jnp.exp2(score - fin_ref[0, g : g + 1, rows])
            ds = (p * (dprob - fin_ref[0, group + g : group + g + 1, rows])).astype(BF16)
            spot = slice(g * tok + i * BLOCK, g * tok + (i + 1) * BLOCK)
            pb_ref[:top, spot] = p.astype(BF16)
            ds_ref[:top, spot] = ds
            dq = dqp_ref[rows, cols] + dot(ds, kh[:top], TN)
            dy = unturn(dq * SCALE, cosv[rows], sinv[rows])
            x = q_ref[rows, cols].astype(F32)
            rstd = inverse_rms(x)
            qpart = qpart + jnp.sum((dy * x * rstd).reshape(BLOCK // 8, 8, dim), axis=0)
            gy = dy * gain
            mean = jnp.mean(gy * x, axis=-1, keepdims=True)
            qg_ref[rows, cols] = (rstd * gy - x * (rstd * rstd * rstd * mean)).astype(BF16)
    kpart = jnp.zeros((8, dim), F32)
    for j in range(tok // BLOCK):
        rows = slice(j * BLOCK, (j + 1) * BLOCK)
        low = j * BLOCK
        dk, dv = 0.0, 0.0
        for g in range(group):
            spot = slice(g * tok + low, (g + 1) * tok)
            cols = slice(g * dim, (g + 1) * dim)
            dk = dk + dot(ds_ref[rows, spot], qh_ref[low:, cols], NN)
            dv = dv + dot(pb_ref[rows, spot], g_ref[low:, cols], NN)
        dy = unturn(dk * LN2, cosv[rows], sinv[rows])
        x = k_ref[rows, :].astype(F32)
        kpart = kpart + jnp.sum((dy * x * inverse_rms(x)).reshape(BLOCK // 8, 8, dim), axis=0)
        dy_ref[rows, :] = dy
        dv_ref[rows, :] = dv
    part_ref[0, 0:8, :] = qpart
    part_ref[0, 8:16, :] = kpart


def finish_kernel(k_ref, dy_ref, dv_ref, dyb_ref, dvb_ref, kgain_ref, kg_ref, vg_ref):
    x = k_ref[...].astype(F32)
    rstd = inverse_rms(x)
    gy = (dy_ref[...] + dyb_ref[...].astype(F32)) * kgain_ref[...]
    mean = jnp.mean(gy * x, axis=-1, keepdims=True)
    kg_ref[...] = (rstd * gy - x * (rstd * rstd * rstd * mean)).astype(BF16)
    vg_ref[...] = (dv_ref[...] + dvb_ref[...].astype(F32)).astype(BF16)


def sum_all(x, work):
    done = None
    for axis in ("seq", "head"):
        size, step = lax.axis_size(axis), 1
        while step < size:
            x = x + lax.ppermute(x, axis, [(i, i ^ step) for i in range(size)])
            if axis == "seq" and step == 2:
                done = work()
                x, done = lax.optimization_barrier((x, done))
            step *= 2
    return x, done


def local(q_raw, k_raw, values, grad_out, segment_ids, q_gain, k_gain):
    tok = q_raw.shape[0]
    dim = q_gain.shape[0]
    q_local = q_raw.shape[1] // dim
    kv_local = k_raw.shape[1] // dim
    group = q_local // kv_local
    devices = lax.axis_size("seq")
    cos, sin, cdev, sdev = tables(tok, devices, dim)
    seg = segment_ids.reshape(devices, tok // 128, 128)
    qgain, kgain = q_gain.reshape(1, dim), k_gain.reshape(1, dim)

    k_prev = shifted(k_raw, "seq", 1)
    v_prev = shifted(values, "seq", 1)

    def whole(a):
        return pl.BlockSpec(a.shape, lambda h: (0,) * a.ndim)

    qspec = pl.BlockSpec((tok, group * dim), lambda h: (0, h))
    kspec = pl.BlockSpec((tok, dim), lambda h: (0, h))
    stat_spec = pl.BlockSpec((1, 8, tok), lambda h: (h, 0, 0))
    stat_shape = jax.ShapeDtypeStruct((kv_local, 8, tok), F32)
    turns = (cos, sin, cdev, sdev)
    turn_specs = [whole(a) for a in turns]
    params = pltpu.CompilerParams(vmem_limit_bytes=60 * 1024 * 1024)
    scratch = [pltpu.VMEM((tok, group * tok), BF16)] * 2

    def cost(products):
        pairs = q_local * tok * tok * 5 // 8
        return pl.CostEstimate(
            flops=2 * products * pairs * dim * 2, bytes_accessed=4 << 20, transcendentals=pairs
        )

    qh, kh, stat = pl.pallas_call(
        stats_kernel,
        grid=(kv_local,),
        in_specs=[qspec, kspec, kspec, qspec, whole(seg), whole(qgain), whole(kgain)] + turn_specs,
        out_specs=[qspec, kspec, stat_spec],
        out_shape=[
            jax.ShapeDtypeStruct(q_raw.shape, BF16),
            jax.ShapeDtypeStruct(k_raw.shape, BF16),
            stat_shape,
        ],
        compiler_params=params,
        cost_estimate=cost(2),
        name="own_statistics",
    )(q_raw, k_raw, values, grad_out, seg, qgain, kgain, *turns)

    dq_prev, dk_prev, dv_prev, fin, kpart_prev = pl.pallas_call(
        halo_kernel,
        grid=(kv_local,),
        in_specs=[qspec, kspec, kspec, qspec, whole(seg), whole(kgain)] + turn_specs + [stat_spec],
        out_specs=[qspec, kspec, kspec, stat_spec, pl.BlockSpec((1, 8, dim), lambda h: (h, 0, 0))],
        out_shape=[
            jax.ShapeDtypeStruct(q_raw.shape, F32),
            jax.ShapeDtypeStruct(k_raw.shape, BF16),
            jax.ShapeDtypeStruct(k_raw.shape, BF16),
            stat_shape,
            jax.ShapeDtypeStruct((kv_local, 8, dim), F32),
        ],
        scratch_shapes=scratch,
        compiler_params=params,
        cost_estimate=cost(5),
        name="previous_keys",
    )(qh, k_prev, v_prev, grad_out, seg, kgain, *turns, stat)

    dy_back = shifted(dk_prev, "seq", -1)
    dv_back = shifted(dv_prev, "seq", -1)

    q_grad, dy_own, dv_own, parts = pl.pallas_call(
        own_kernel,
        grid=(kv_local,),
        in_specs=[qspec, kspec, kspec, qspec, qspec, kspec, whole(seg), whole(qgain)]
        + turn_specs
        + [stat_spec, qspec],
        out_specs=[qspec, kspec, kspec, pl.BlockSpec((1, 16, dim), lambda h: (h, 0, 0))],
        out_shape=[
            jax.ShapeDtypeStruct(q_raw.shape, BF16),
            jax.ShapeDtypeStruct(k_raw.shape, F32),
            jax.ShapeDtypeStruct(k_raw.shape, F32),
            jax.ShapeDtypeStruct((kv_local, 16, dim), F32),
        ],
        scratch_shapes=scratch,
        compiler_params=params,
        cost_estimate=cost(5),
        name="own_keys",
    )(qh, kh, values, grad_out, q_raw, k_raw, seg, qgain, *turns, fin, dq_prev)

    sums = jnp.stack(
        [jnp.sum(parts[:, :8], axis=(0, 1)), jnp.sum(parts[:, 8:], axis=(0, 1)) + jnp.sum(kpart_prev, axis=(0, 1))]
    )
    sums, dy_back, dv_back = lax.optimization_barrier((sums, dy_back, dv_back))

    finish = pl.pallas_call(
        finish_kernel,
        grid=(kv_local,),
        in_specs=[kspec] * 5 + [whole(kgain)],
        out_specs=[kspec, kspec],
        out_shape=[jax.ShapeDtypeStruct(k_raw.shape, BF16)] * 2,
        compiler_params=params,
        cost_estimate=pl.CostEstimate(flops=1 << 20, bytes_accessed=5 << 20, transcendentals=0),
        name="add_returned",
    )
    sums, (k_grad, v_grad) = sum_all(
        sums, lambda: finish(k_raw, dy_own, dv_own, dy_back, dv_back, kgain)
    )
    return (q_grad, k_grad, v_grad, sums[0], sums[1])


def solution(mesh):
    in_specs = (
        P("seq", "head"),
        P("seq", "head"),
        P("seq", "head"),
        P("seq", "head"),
        P(),
        P(),
        P(),
    )
    out_specs = (P("seq", "head"), P("seq", "head"), P("seq", "head"), P(), P())
    return jax.shard_map(local, mesh=mesh, in_specs=in_specs, out_specs=out_specs, check_vma=False)
```

```python
import functools

import jax
import jax.numpy as jnp
import numpy as np
from jax import lax
from jax.experimental import pallas as pl
from jax.experimental.pallas import tpu as pltpu
from jax.sharding import PartitionSpec as P

WINDOW = 1024
BLOCK = 256
SCALE = 168.0 ** (-0.5)
EPS = 1e-06
BASE = 10000.0
LOG2E = 1.4426950408889634
LN2 = 0.6931471805599453
NEG = -1e30
APART = -32768.0
DOCS = 32
F32 = jnp.float32
BF16 = jnp.bfloat16
NT = (((1,), (1,)), ((), ()))
NN = (((1,), (0,)), ((), ()))
TN = (((0,), (0,)), ((), ()))


def shifted(block, axis, distance):
    devices = range(lax.axis_size(axis))
    route = [(i - distance, i) for i in devices if i - distance in devices]
    return lax.ppermute(block, axis, route)


def tables(tok, devices, dim):
    half = dim // 2
    freq = BASE ** (-np.arange(half, dtype=np.float64) * 2.0 / dim)
    freq = np.concatenate([freq, freq])
    sign = np.concatenate([-np.ones(half), np.ones(half)])
    inner = np.arange(tok, dtype=np.float64)[:, None] * freq
    rows = -(-(devices + 1) // 8) * 8
    outer = (np.arange(rows, dtype=np.float64)[:, None] - 1.0) * tok * freq
    return tuple(
        np.asarray(a, np.float32)
        for a in (np.cos(inner), np.sin(inner) * sign, np.cos(outer), np.sin(outer) * sign)
    )


def dot(a, b, dims):
    return lax.dot_general(a, b, dims, preferred_element_type=F32)


def turn(cos_ref, sin_ref, cdev_ref, sdev_ref, row):
    cl, sl = cos_ref[...], sin_ref[...]
    cd, sd = cdev_ref[pl.ds(row, 1), :], sdev_ref[pl.ds(row, 1), :]
    return cl * cd - sl * sd, sl * cd + cl * sd


def swap(y):
    return pltpu.roll(y, y.shape[-1] // 2, 1)


def inverse_rms(x):
    return lax.rsqrt(jnp.mean(x * x, axis=-1, keepdims=True) + EPS)


def normed(raw, gain, cosv, sinv):
    x = raw.astype(F32)
    y = x * inverse_rms(x) * gain
    return (y * cosv + swap(y) * sinv).astype(BF16)


def unturn(g, cosv, sinv):
    return g * cosv - swap(g) * sinv


def doc_rows(seg):
    row = jnp.concatenate([seg[i : i + 1, :] for i in range(seg.shape[0])], axis=1)
    ids = lax.broadcasted_iota(jnp.int32, (DOCS, row.shape[1]), 0)
    return jnp.where(ids == row, 1.0, 0.0).T


def query_side(onehot):
    return ((1.0 - onehot) * APART).astype(BF16)


def corner(strict, repeat=1):
    k = lax.broadcasted_iota(jnp.int32, (BLOCK, BLOCK), 0)
    q = lax.broadcasted_iota(jnp.int32, (BLOCK, BLOCK), 1)
    inside = jnp.where(k > q if strict else k <= q, 1, 0)
    return jnp.concatenate([inside] * repeat, axis=1) > 0


def masked_tail(score, inside):
    edge = score.shape[0] - BLOCK
    if edge == 0:
        return jnp.where(inside, score, NEG)
    return jnp.concatenate([score[:edge], jnp.where(inside, score[edge:], NEG)], axis=0)


def masked_head(score, inside):
    if score.shape[0] == BLOCK:
        return jnp.where(inside, score, NEG)
    return jnp.concatenate([jnp.where(inside, score[:BLOCK], NEG), score[BLOCK:]], axis=0)


def add_up(ref, low, value, fresh):
    for j in range(value.shape[0] // BLOCK):
        rows, part = pl.ds(low + j * BLOCK, BLOCK), value[j * BLOCK : (j + 1) * BLOCK]
        ref[rows, :] = part if j == fresh else ref[rows, :] + part


def heads(ref, rows, group):
    dim = ref.shape[1] // group
    return jnp.concatenate([ref[rows, g * dim : (g + 1) * dim] for g in range(group)], axis=0)


def query_rows(ref, first, rows, group):
    return jnp.concatenate([ref[0, first + g : first + g + 1, rows] for g in range(group)], axis=1)


def stats_kernel(
    q_ref, k_ref, v_ref, g_ref, seg_ref, qgain_ref, kgain_ref, cos_ref, sin_ref, cdev_ref, sdev_ref,
    qh_ref, kh_ref, stat_ref, cosv_ref, sinv_ref, kdoc_ref, qt_ref, gt_ref,
):
    tok, dim = k_ref.shape
    group = q_ref.shape[1] // dim

    @pl.when(pl.program_id(0) == 0)
    def _():
        s = lax.axis_index("seq")
        cosv_ref[...], sinv_ref[...] = turn(cos_ref, sin_ref, cdev_ref, sdev_ref, s + 1)
        onehot = doc_rows(seg_ref[pl.ds(s, 1)][0])
        kdoc_ref[...] = onehot.astype(BF16)
        qt_ref[dim:, :] = query_side(onehot).T

    cosv, sinv = cosv_ref[...], sinv_ref[...]
    kh = normed(k_ref[...], kgain_ref[...], cosv, sinv)
    kh_ref[...] = kh
    kside = jnp.concatenate([kh, kdoc_ref[...]], axis=1)
    inside = corner(False)
    for g in range(group):
        cols = slice(g * dim, (g + 1) * dim)
        qh = normed(q_ref[:, cols], qgain_ref[...] * (SCALE * LOG2E), cosv, sinv)
        qh_ref[:, cols] = qh
        qt_ref[:dim, :] = qh.T
        gt_ref[...] = g_ref[:, cols].T
        for i in range(tok // BLOCK):
            rows = slice(i * BLOCK, (i + 1) * BLOCK)
            top = (i + 1) * BLOCK
            score = masked_tail(dot(kside[:top], qt_ref[:, rows], NN), inside)
            dprob = dot(v_ref[:top, :], gt_ref[:, rows], NN)
            m = jnp.max(score, axis=0, keepdims=True)
            e = jnp.exp2(score - m)
            stat_ref[0, g : g + 1, rows] = m
            stat_ref[0, group + g : group + g + 1, rows] = jnp.sum(e, axis=0, keepdims=True)
            stat_ref[0, 2 * group + g : 2 * group + g + 1, rows] = jnp.sum(e * dprob, axis=0, keepdims=True)


def halo_kernel(
    qh_ref, k_ref, v_ref, g_ref, seg_ref, kgain_ref, cos_ref, sin_ref, cdev_ref, sdev_ref, stat_ref,
    dq_ref, back_ref, fin_ref, part_ref, cosv_ref, sinv_ref, kdoc_ref, qdoc_ref, dka_ref, dva_ref,
):
    tok, dim = k_ref.shape
    group = qh_ref.shape[1] // dim

    @pl.when(pl.program_id(0) == 0)
    def _():
        s = lax.axis_index("seq")
        cosv_ref[...], sinv_ref[...] = turn(cos_ref, sin_ref, cdev_ref, sdev_ref, s)
        qdoc_ref[...] = query_side(doc_rows(seg_ref[pl.ds(s, 1)][0]))
        before = doc_rows(seg_ref[pl.ds(jnp.maximum(s - 1, 0), 1)][0])
        kdoc_ref[...] = jnp.where(s == 0, 1.0, before).astype(BF16)

    cosv, sinv = cosv_ref[...], sinv_ref[...]
    qdoc = qdoc_ref[...]
    kh = normed(k_ref[...], kgain_ref[...], cosv, sinv)
    kside = jnp.concatenate([kh, kdoc_ref[...]], axis=1)
    inside = corner(True, group)

    def products(i):
        rows, low = slice(i * BLOCK, (i + 1) * BLOCK), i * BLOCK
        qside = jnp.concatenate([heads(qh_ref, rows, group), jnp.concatenate([qdoc[rows]] * group, axis=0)], axis=1)
        return dot(kside[low:], qside, NT), dot(v_ref[low:, :], heads(g_ref, rows, group), NT)

    def soft(i, score, dprob):
        rows = slice(i * BLOCK, (i + 1) * BLOCK)
        score = masked_head(score, inside)
        m_own = query_rows(stat_ref, 0, rows, group)
        m = jnp.maximum(m_own, jnp.max(score, axis=0, keepdims=True))
        e = jnp.exp2(score - m)
        keep = jnp.exp2(m_own - m)
        total = query_rows(stat_ref, group, rows, group) * keep + jnp.sum(e, axis=0, keepdims=True)
        moment = query_rows(stat_ref, 2 * group, rows, group) * keep + jnp.sum(e * dprob, axis=0, keepdims=True)
        inv = 1.0 / total
        delta = moment * inv
        lse = m + jnp.log2(total)
        for g in range(group):
            spot = slice(g * BLOCK, (g + 1) * BLOCK)
            fin_ref[0, g : g + 1, rows] = lse[:, spot]
            fin_ref[0, group + g : group + g + 1, rows] = delta[:, spot]
        p = e * inv
        return p.astype(BF16), (p * (dprob - delta)).astype(BF16)

    def grads(i, pb, ds):
        rows, low = slice(i * BLOCK, (i + 1) * BLOCK), i * BLOCK
        dq = dot(ds, kh[low:], TN)
        for g in range(group):
            dq_ref[rows, g * dim : (g + 1) * dim] = dq[g * BLOCK : (g + 1) * BLOCK]
        add_up(dka_ref, low, dot(ds, heads(qh_ref, rows, group), NN), 0)
        add_up(dva_ref, low, dot(pb, heads(g_ref, rows, group), NN), 0)

    run_units(reversed(range(tok // BLOCK)), products, soft, grads)
    part = jnp.zeros((8, dim), F32)
    for j in range(tok // BLOCK):
        rows = slice(j * BLOCK, (j + 1) * BLOCK)
        dy = unturn(dka_ref[rows, :] * LN2, cosv[rows], sinv[rows])
        x = k_ref[rows, :].astype(F32)
        part = part + jnp.sum((dy * x * inverse_rms(x)).reshape(BLOCK // 8, 8, dim), axis=0)
        back_ref[rows, :dim] = dy.astype(BF16)
        back_ref[rows, dim:] = dva_ref[rows, :].astype(BF16)
    part_ref[0] = part


def run_units(units, products, soft, grads):
    waiting = None
    for unit in units:
        made = products(unit)
        if waiting is not None:
            grads(*waiting)
        waiting = (unit, *soft(unit, *made))
    grads(*waiting)


def own_kernel(
    qh_ref, kh_ref, v_ref, g_ref, q_ref, k_ref, seg_ref, qgain_ref, cos_ref, sin_ref, cdev_ref, sdev_ref,
    fin_ref, dqp_ref, kpart_ref, qg_ref, dy_ref, dv_ref, sums_ref, cosv_ref, sinv_ref, kdoc_ref, qdoc_ref, dka_ref, part_ref,
):
    tok, dim = kh_ref.shape
    group = qh_ref.shape[1] // dim

    @pl.when(pl.program_id(0) == 0)
    def _():
        s = lax.axis_index("seq")
        cosv_ref[...], sinv_ref[...] = turn(cos_ref, sin_ref, cdev_ref, sdev_ref, s + 1)
        onehot = doc_rows(seg_ref[pl.ds(s, 1)][0])
        kdoc_ref[...] = onehot.astype(BF16)
        qdoc_ref[...] = query_side(onehot)
        part_ref[...] = jnp.zeros_like(part_ref)

    cosv, sinv = cosv_ref[...], sinv_ref[...]
    qdoc = qdoc_ref[...]
    kh = kh_ref[...]
    kside = jnp.concatenate([kh, kdoc_ref[...]], axis=1)
    inside = corner(False, group)
    gain = qgain_ref[...]

    def products(i):
        rows, top = slice(i * BLOCK, (i + 1) * BLOCK), (i + 1) * BLOCK
        qside = jnp.concatenate([heads(qh_ref, rows, group), jnp.concatenate([qdoc[rows]] * group, axis=0)], axis=1)
        return dot(kside[:top], qside, NT), dot(v_ref[:top, :], heads(g_ref, rows, group), NT)

    def soft(i, score, dprob):
        rows = slice(i * BLOCK, (i + 1) * BLOCK)
        p = jnp.exp2(masked_tail(score, inside) - query_rows(fin_ref, 0, rows, group))
        ds = p * (dprob - query_rows(fin_ref, group, rows, group))
        return p.astype(BF16), ds.astype(BF16)

    def grads(i, pb, ds):
        rows, top = slice(i * BLOCK, (i + 1) * BLOCK), (i + 1) * BLOCK
        dq_own = dot(ds, kh[:top], TN)
        add_up(dka_ref, 0, dot(ds, heads(qh_ref, rows, group), NN), i)
        add_up(dv_ref, 0, dot(pb, heads(g_ref, rows, group), NN), i)
        for g in range(group):
            cols = slice(g * dim, (g + 1) * dim)
            dq = dqp_ref[rows, cols] + dq_own[g * BLOCK : (g + 1) * BLOCK]
            dy = unturn(dq * SCALE, cosv[rows], sinv[rows])
            x = q_ref[rows, cols].astype(F32)
            rstd = inverse_rms(x)
            part_ref[0] += jnp.sum((dy * x * rstd).reshape(BLOCK // 8, 8, dim), axis=0)
            gy = dy * gain
            mean = jnp.mean(gy * x, axis=-1, keepdims=True)
            qg_ref[rows, cols] = (rstd * gy - x * (rstd * rstd * rstd * mean)).astype(BF16)

    run_units(range(tok // BLOCK), products, soft, grads)
    kpart = kpart_ref[0]
    for j in range(tok // BLOCK):
        rows = slice(j * BLOCK, (j + 1) * BLOCK)
        dy = unturn(dka_ref[rows, :] * LN2, cosv[rows], sinv[rows])
        x = k_ref[rows, :].astype(F32)
        kpart = kpart + jnp.sum((dy * x * inverse_rms(x)).reshape(BLOCK // 8, 8, dim), axis=0)
        dy_ref[rows, :] = dy
    part_ref[1] += kpart
    sums_ref[...] = jnp.concatenate([jnp.sum(part_ref[n], axis=0, keepdims=True) for n in range(2)], axis=0)


def finish_kernel(k_ref, dy_ref, dv_ref, back_ref, kgain_ref, kg_ref, vg_ref):
    dim = k_ref.shape[1]
    x = k_ref[...].astype(F32)
    rstd = inverse_rms(x)
    gy = (dy_ref[...] + back_ref[:, :dim].astype(F32)) * kgain_ref[...]
    mean = jnp.mean(gy * x, axis=-1, keepdims=True)
    kg_ref[...] = (rstd * gy - x * (rstd * rstd * rstd * mean)).astype(BF16)
    vg_ref[...] = (dv_ref[...] + back_ref[:, dim:].astype(F32)).astype(BF16)


def pairwise(x, axis, step):
    return x + lax.ppermute(x, axis, [(i, i ^ step) for i in range(lax.axis_size(axis))])


def local(q_raw, k_raw, values, grad_out, segment_ids, q_gain, k_gain):
    tok = q_raw.shape[0]
    dim = q_gain.shape[0]
    q_local = q_raw.shape[1] // dim
    kv_local = k_raw.shape[1] // dim
    group = q_local // kv_local
    devices = lax.axis_size("seq")
    cos, sin, cdev, sdev = tables(tok, devices, dim)
    seg = segment_ids.reshape(devices, tok // 128, 128)
    qgain, kgain = q_gain.reshape(1, dim), k_gain.reshape(1, dim)

    k_prev = shifted(k_raw, "seq", 1)
    v_prev = shifted(values, "seq", 1)

    def whole(a):
        return pl.BlockSpec(a.shape, lambda h: (0,) * a.ndim)

    qspec = pl.BlockSpec((tok, group * dim), lambda h: (0, h))
    kspec = pl.BlockSpec((tok, dim), lambda h: (0, h))
    pair_spec = pl.BlockSpec((tok, 2 * dim), lambda h: (0, h))
    stat_spec = pl.BlockSpec((1, 8, tok), lambda h: (h, 0, 0))
    stat_shape = jax.ShapeDtypeStruct((kv_local, 8, tok), F32)
    turns = (cos, sin, cdev, sdev)
    turn_specs = [whole(a) for a in turns]
    params = pltpu.CompilerParams(vmem_limit_bytes=60 * 1024 * 1024)
    roomy = pltpu.CompilerParams(vmem_limit_bytes=57 * 1024 * 1024)
    part_spec = pl.BlockSpec((1, 8, dim), lambda h: (h, 0, 0))
    prep = [pltpu.VMEM((tok, dim), F32)] * 2 + [pltpu.VMEM((tok, DOCS), BF16)] * 2
    total = pltpu.VMEM((tok, dim), F32)

    def cost(products):
        pairs = q_local * tok * tok * 5 // 8
        return pl.CostEstimate(
            flops=2 * products * pairs * dim * 2, bytes_accessed=4 << 20, transcendentals=pairs
        )

    qh, kh, stat = pl.pallas_call(
        stats_kernel,
        grid=(kv_local,),
        in_specs=[qspec, kspec, kspec, qspec, whole(seg), whole(qgain), whole(kgain)] + turn_specs,
        out_specs=[qspec, kspec, stat_spec],
        out_shape=[
            jax.ShapeDtypeStruct(q_raw.shape, BF16),
            jax.ShapeDtypeStruct(k_raw.shape, BF16),
            stat_shape,
        ],
        scratch_shapes=prep[:3] + [pltpu.VMEM((dim + DOCS, tok), BF16), pltpu.VMEM((dim, tok), BF16)],
        compiler_params=params,
        cost_estimate=cost(2),
        name="own_statistics",
    )(q_raw, k_raw, values, grad_out, seg, qgain, kgain, *turns)

    dq_prev, back, fin, kpart_prev = pl.pallas_call(
        halo_kernel,
        grid=(kv_local,),
        in_specs=[qspec, kspec, kspec, qspec, whole(seg), whole(kgain)] + turn_specs + [stat_spec],
        out_specs=[qspec, pair_spec, stat_spec, part_spec],
        out_shape=[
            jax.ShapeDtypeStruct(q_raw.shape, F32),
            jax.ShapeDtypeStruct((tok, 2 * kv_local * dim), BF16),
            stat_shape,
            jax.ShapeDtypeStruct((kv_local, 8, dim), F32),
        ],
        scratch_shapes=prep + [total, total],
        compiler_params=roomy,
        cost_estimate=cost(5),
        name="previous_keys",
    )(qh, k_prev, v_prev, grad_out, seg, kgain, *turns, stat)

    back = shifted(back, "seq", -1)

    q_grad, dy_own, dv_own, sums = pl.pallas_call(
        own_kernel,
        grid=(kv_local,),
        in_specs=[qspec, kspec, kspec, qspec, qspec, kspec, whole(seg), whole(qgain)]
        + turn_specs
        + [stat_spec, qspec, part_spec],
        out_specs=[qspec, kspec, kspec, pl.BlockSpec((2, dim), lambda h: (0, 0))],
        out_shape=[
            jax.ShapeDtypeStruct(q_raw.shape, BF16),
            jax.ShapeDtypeStruct(k_raw.shape, F32),
            jax.ShapeDtypeStruct(k_raw.shape, F32),
            jax.ShapeDtypeStruct((2, dim), F32),
        ],
        scratch_shapes=prep + [total, pltpu.VMEM((2, 8, dim), F32)],
        compiler_params=params,
        cost_estimate=cost(5),
        name="own_keys",
    )(qh, kh, values, grad_out, q_raw, k_raw, seg, qgain, *turns, fin, dq_prev, kpart_prev)

    finish = pl.pallas_call(
        finish_kernel,
        grid=(kv_local,),
        in_specs=[kspec] * 3 + [pair_spec, whole(kgain)],
        out_specs=[kspec, kspec],
        out_shape=[jax.ShapeDtypeStruct(k_raw.shape, BF16)] * 2,
        compiler_params=roomy,
        cost_estimate=pl.CostEstimate(flops=1 << 20, bytes_accessed=5 << 20, transcendentals=0),
        name="add_returned",
    )
    for step in (("head", 1), ("head", 2), ("seq", 1)):
        sums = pairwise(sums, *step)
    sums, back = lax.optimization_barrier((sums, back))
    for step in (("seq", 2), ("seq", 4), ("seq", 8), ("seq", 16), ("head", 4)):
        sums = pairwise(sums, *step)
        if step == ("seq", 8):
            sums, (k_grad, v_grad) = lax.optimization_barrier(
                (sums, finish(k_raw, dy_own, dv_own, back, kgain))
            )
    return (q_grad, k_grad, v_grad, sums[0], sums[1])


def solution(mesh):
    in_specs = (
        P("seq", "head"),
        P("seq", "head"),
        P("seq", "head"),
        P("seq", "head"),
        P(),
        P(),
        P(),
    )
    out_specs = (P("seq", "head"), P("seq", "head"), P("seq", "head"), P(), P())
    return jax.shard_map(local, mesh=mesh, in_specs=in_specs, out_specs=out_specs, check_vma=False)
```

```python
import functools

import jax
import jax.numpy as jnp
import numpy as np
from jax import lax
from jax.experimental import pallas as pl
from jax.experimental.pallas import tpu as pltpu
from jax.sharding import PartitionSpec as P

WINDOW = 1024
BLOCK = 256
SCALE = 168.0 ** (-0.5)
EPS = 1e-06
BASE = 10000.0
LOG2E = 1.4426950408889634
LN2 = 0.6931471805599453
NEG = -1e30
APART = -32768.0
DOCS = 32
F32 = jnp.float32
BF16 = jnp.bfloat16
NT = (((1,), (1,)), ((), ()))
NN = (((1,), (0,)), ((), ()))
TN = (((0,), (0,)), ((), ()))


def shifted(block, axis, distance):
    devices = range(lax.axis_size(axis))
    route = [(i - distance, i) for i in devices if i - distance in devices]
    return lax.ppermute(block, axis, route)


def tables(tok, devices, dim):
    half = dim // 2
    freq = BASE ** (-np.arange(half, dtype=np.float64) * 2.0 / dim)
    freq = np.concatenate([freq, freq])
    sign = np.concatenate([-np.ones(half), np.ones(half)])
    inner = np.arange(tok, dtype=np.float64)[:, None] * freq
    rows = -(-(devices + 1) // 8) * 8
    outer = (np.arange(rows, dtype=np.float64)[:, None] - 1.0) * tok * freq
    return tuple(
        np.asarray(a, np.float32)
        for a in (np.cos(inner), np.sin(inner) * sign, np.cos(outer), np.sin(outer) * sign)
    )


def dot(a, b, dims):
    return lax.dot_general(a, b, dims, preferred_element_type=F32)


def turn(cos_ref, sin_ref, cdev_ref, sdev_ref, row):
    cl, sl = cos_ref[...], sin_ref[...]
    cd, sd = cdev_ref[pl.ds(row, 1), :], sdev_ref[pl.ds(row, 1), :]
    return cl * cd - sl * sd, sl * cd + cl * sd


def swap(y):
    return pltpu.roll(y, y.shape[-1] // 2, 1)


def inverse_rms(x):
    return lax.rsqrt(jnp.mean(x * x, axis=-1, keepdims=True) + EPS)


def normed(raw, gain, cosv, sinv):
    x = raw.astype(F32)
    y = x * inverse_rms(x) * gain
    return (y * cosv + swap(y) * sinv).astype(BF16)


def unturn(g, cosv, sinv):
    return g * cosv - swap(g) * sinv


def doc_rows(seg):
    row = jnp.concatenate([seg[i : i + 1, :] for i in range(seg.shape[0])], axis=1)
    ids = lax.broadcasted_iota(jnp.int32, (DOCS, row.shape[1]), 0)
    return jnp.where(ids == row, 1.0, 0.0).T


def query_side(onehot):
    return ((1.0 - onehot) * APART).astype(BF16)


def corner(strict, repeat=1):
    k = lax.broadcasted_iota(jnp.int32, (BLOCK, BLOCK), 0)
    q = lax.broadcasted_iota(jnp.int32, (BLOCK, BLOCK), 1)
    inside = jnp.where(k > q if strict else k <= q, 1, 0)
    return jnp.concatenate([inside] * repeat, axis=1) > 0


def masked_tail(score, inside):
    edge = score.shape[0] - BLOCK
    if edge == 0:
        return jnp.where(inside, score, NEG)
    return jnp.concatenate([score[:edge], jnp.where(inside, score[edge:], NEG)], axis=0)


def masked_head(score, inside):
    if score.shape[0] == BLOCK:
        return jnp.where(inside, score, NEG)
    return jnp.concatenate([jnp.where(inside, score[:BLOCK], NEG), score[BLOCK:]], axis=0)


def add_up(ref, low, value, fresh):
    for j in range(value.shape[0] // BLOCK):
        rows, part = pl.ds(low + j * BLOCK, BLOCK), value[j * BLOCK : (j + 1) * BLOCK]
        ref[rows, :] = part if j == fresh else ref[rows, :] + part


def heads(ref, rows, group):
    dim = ref.shape[1] // group
    return jnp.concatenate([ref[rows, g * dim : (g + 1) * dim] for g in range(group)], axis=0)


def query_rows(ref, first, rows, group):
    return jnp.concatenate([ref[0, first + g : first + g + 1, rows] for g in range(group)], axis=1)


def stats_kernel(
    q_ref, k_ref, v_ref, g_ref, seg_ref, qgain_ref, kgain_ref, cos_ref, sin_ref, cdev_ref, sdev_ref,
    qh_ref, kh_ref, stat_ref, kdoc_ref, qdoc_ref, cosv_ref, sinv_ref, qt_ref, gt_ref,
):
    tok, dim = k_ref.shape
    group = q_ref.shape[1] // dim

    @pl.when(pl.program_id(0) == 0)
    def _():
        s = lax.axis_index("seq")
        cosv_ref[...], sinv_ref[...] = turn(cos_ref, sin_ref, cdev_ref, sdev_ref, s + 1)
        onehot = doc_rows(seg_ref[pl.ds(s, 1)][0])
        kdoc_ref[...] = onehot.astype(BF16)
        qdoc_ref[...] = query_side(onehot)
        qt_ref[dim:, :] = qdoc_ref[...].T

    cosv, sinv = cosv_ref[...], sinv_ref[...]
    kh = normed(k_ref[...], kgain_ref[...], cosv, sinv)
    kh_ref[...] = kh
    kside = jnp.concatenate([kh, kdoc_ref[...]], axis=1)
    inside = corner(False)
    for g in range(group):
        cols = slice(g * dim, (g + 1) * dim)
        qh = normed(q_ref[:, cols], qgain_ref[...] * (SCALE * LOG2E), cosv, sinv)
        qh_ref[:, cols] = qh
        qt_ref[:dim, :] = qh.T
        gt_ref[...] = g_ref[:, cols].T
        for i in range(tok // BLOCK):
            rows = slice(i * BLOCK, (i + 1) * BLOCK)
            top = (i + 1) * BLOCK
            score = masked_tail(dot(kside[:top], qt_ref[:, rows], NN), inside)
            dprob = dot(v_ref[:top, :], gt_ref[:, rows], NN)
            m = jnp.max(score, axis=0, keepdims=True)
            e = jnp.exp2(score - m)
            stat_ref[0, g : g + 1, rows] = m
            stat_ref[0, group + g : group + g + 1, rows] = jnp.sum(e, axis=0, keepdims=True)
            stat_ref[0, 2 * group + g : 2 * group + g + 1, rows] = jnp.sum(e * dprob, axis=0, keepdims=True)


def halo_kernel(
    qh_ref, k_ref, v_ref, g_ref, seg_ref, qdoc_ref, kgain_ref, cos_ref, sin_ref, cdev_ref, sdev_ref, stat_ref,
    dq_ref, back_ref, fin_ref, part_ref, cosv_ref, sinv_ref, kdoc_ref, dka_ref, dva_ref,
):
    tok, dim = k_ref.shape
    group = qh_ref.shape[1] // dim

    @pl.when(pl.program_id(0) == 0)
    def _():
        s = lax.axis_index("seq")
        cosv_ref[...], sinv_ref[...] = turn(cos_ref, sin_ref, cdev_ref, sdev_ref, s)
        before = doc_rows(seg_ref[pl.ds(jnp.maximum(s - 1, 0), 1)][0])
        kdoc_ref[...] = jnp.where(s == 0, 1.0, before).astype(BF16)

    cosv, sinv = cosv_ref[...], sinv_ref[...]
    qdoc = qdoc_ref[...]
    kh = normed(k_ref[...], kgain_ref[...], cosv, sinv)
    kside = jnp.concatenate([kh, kdoc_ref[...]], axis=1)
    inside = corner(True, group)

    def products(i):
        rows, low = slice(i * BLOCK, (i + 1) * BLOCK), i * BLOCK
        qside = jnp.concatenate([heads(qh_ref, rows, group), jnp.concatenate([qdoc[rows]] * group, axis=0)], axis=1)
        return dot(kside[low:], qside, NT), dot(v_ref[low:, :], heads(g_ref, rows, group), NT)

    def soft(i, score, dprob):
        rows = slice(i * BLOCK, (i + 1) * BLOCK)
        score = masked_head(score, inside)
        m_own = query_rows(stat_ref, 0, rows, group)
        m = jnp.maximum(m_own, jnp.max(score, axis=0, keepdims=True))
        e = jnp.exp2(score - m)
        keep = jnp.exp2(m_own - m)
        total = query_rows(stat_ref, group, rows, group) * keep + jnp.sum(e, axis=0, keepdims=True)
        moment = query_rows(stat_ref, 2 * group, rows, group) * keep + jnp.sum(e * dprob, axis=0, keepdims=True)
        inv = 1.0 / total
        delta = moment * inv
        lse = m + jnp.log2(total)
        for g in range(group):
            spot = slice(g * BLOCK, (g + 1) * BLOCK)
            fin_ref[0, g : g + 1, rows] = lse[:, spot]
            fin_ref[0, group + g : group + g + 1, rows] = delta[:, spot]
        p = e * inv
        return p.astype(BF16), (p * (dprob - delta)).astype(BF16)

    def grads(i, pb, ds):
        rows, low = slice(i * BLOCK, (i + 1) * BLOCK), i * BLOCK
        dq = dot(ds, kh[low:], TN)
        for g in range(group):
            dq_ref[rows, g * dim : (g + 1) * dim] = dq[g * BLOCK : (g + 1) * BLOCK]
        add_up(dka_ref, low, dot(ds, heads(qh_ref, rows, group), NN), 0)
        add_up(dva_ref, low, dot(pb, heads(g_ref, rows, group), NN), 0)

    run_units(reversed(range(tok // BLOCK)), products, soft, grads)
    part = jnp.zeros((8, dim), F32)
    for j in range(tok // BLOCK):
        rows = slice(j * BLOCK, (j + 1) * BLOCK)
        dy = unturn(dka_ref[rows, :] * LN2, cosv[rows], sinv[rows])
        x = k_ref[rows, :].astype(F32)
        part = part + jnp.sum((dy * x * inverse_rms(x)).reshape(BLOCK // 8, 8, dim), axis=0)
        back_ref[rows, :dim] = dy.astype(BF16)
        back_ref[rows, dim:] = dva_ref[rows, :].astype(BF16)
    part_ref[0] = part


def run_units(units, products, soft, grads):
    waiting = None
    for unit in units:
        made = products(unit)
        if waiting is not None:
            grads(*waiting)
        waiting = (unit, *soft(unit, *made))
    grads(*waiting)


def own_kernel(
    qh_ref, kh_ref, v_ref, g_ref, q_ref, k_ref, kdoc_ref, qdoc_ref, qgain_ref, cos_ref, sin_ref, cdev_ref, sdev_ref,
    fin_ref, dqp_ref, kpart_ref, qg_ref, dy_ref, dv_ref, sums_ref, cosv_ref, sinv_ref, dka_ref, part_ref,
):
    tok, dim = kh_ref.shape
    group = qh_ref.shape[1] // dim

    @pl.when(pl.program_id(0) == 0)
    def _():
        s = lax.axis_index("seq")
        cosv_ref[...], sinv_ref[...] = turn(cos_ref, sin_ref, cdev_ref, sdev_ref, s + 1)
        part_ref[...] = jnp.zeros_like(part_ref)

    cosv, sinv = cosv_ref[...], sinv_ref[...]
    qdoc = qdoc_ref[...]
    kh = kh_ref[...]
    kside = jnp.concatenate([kh, kdoc_ref[...]], axis=1)
    inside = corner(False, group)
    gain = qgain_ref[...]

    def products(i):
        rows, top = slice(i * BLOCK, (i + 1) * BLOCK), (i + 1) * BLOCK
        qside = jnp.concatenate([heads(qh_ref, rows, group), jnp.concatenate([qdoc[rows]] * group, axis=0)], axis=1)
        return dot(kside[:top], qside, NT), dot(v_ref[:top, :], heads(g_ref, rows, group), NT)

    def soft(i, score, dprob):
        rows = slice(i * BLOCK, (i + 1) * BLOCK)
        p = jnp.exp2(masked_tail(score, inside) - query_rows(fin_ref, 0, rows, group))
        ds = p * (dprob - query_rows(fin_ref, group, rows, group))
        return p.astype(BF16), ds.astype(BF16)

    def grads(i, pb, ds):
        rows, top = slice(i * BLOCK, (i + 1) * BLOCK), (i + 1) * BLOCK
        dq_own = dot(ds, kh[:top], TN)
        add_up(dka_ref, 0, dot(ds, heads(qh_ref, rows, group), NN), i)
        add_up(dv_ref, 0, dot(pb, heads(g_ref, rows, group), NN), i)
        for g in range(group):
            cols = slice(g * dim, (g + 1) * dim)
            dq = dqp_ref[rows, cols] + dq_own[g * BLOCK : (g + 1) * BLOCK]
            dy = unturn(dq * SCALE, cosv[rows], sinv[rows])
            x = q_ref[rows, cols].astype(F32)
            rstd = inverse_rms(x)
            part_ref[0] += jnp.sum((dy * x * rstd).reshape(BLOCK // 8, 8, dim), axis=0)
            gy = dy * gain
            mean = jnp.mean(gy * x, axis=-1, keepdims=True)
            qg_ref[rows, cols] = (rstd * gy - x * (rstd * rstd * rstd * mean)).astype(BF16)

    run_units(range(tok // BLOCK), products, soft, grads)
    kpart = kpart_ref[0]
    for j in range(tok // BLOCK):
        rows = slice(j * BLOCK, (j + 1) * BLOCK)
        dy = unturn(dka_ref[rows, :] * LN2, cosv[rows], sinv[rows])
        x = k_ref[rows, :].astype(F32)
        kpart = kpart + jnp.sum((dy * x * inverse_rms(x)).reshape(BLOCK // 8, 8, dim), axis=0)
        dy_ref[rows, :] = dy
    part_ref[1] += kpart
    sums_ref[...] = jnp.concatenate([jnp.sum(part_ref[n], axis=0, keepdims=True) for n in range(2)], axis=0)


def finish_kernel(k_ref, dy_ref, dv_ref, back_ref, kgain_ref, kg_ref, vg_ref):
    dim = k_ref.shape[1]
    x = k_ref[...].astype(F32)
    rstd = inverse_rms(x)
    gy = (dy_ref[...] + back_ref[:, :dim].astype(F32)) * kgain_ref[...]
    mean = jnp.mean(gy * x, axis=-1, keepdims=True)
    kg_ref[...] = (rstd * gy - x * (rstd * rstd * rstd * mean)).astype(BF16)
    vg_ref[...] = (dv_ref[...] + back_ref[:, dim:].astype(F32)).astype(BF16)


def pairwise(x, axis, step):
    return x + lax.ppermute(x, axis, [(i, i ^ step) for i in range(lax.axis_size(axis))])


def local(q_raw, k_raw, values, grad_out, segment_ids, q_gain, k_gain):
    tok = q_raw.shape[0]
    dim = q_gain.shape[0]
    q_local = q_raw.shape[1] // dim
    kv_local = k_raw.shape[1] // dim
    group = q_local // kv_local
    devices = lax.axis_size("seq")
    cos, sin, cdev, sdev = tables(tok, devices, dim)
    seg = segment_ids.reshape(devices, tok // 128, 128)
    qgain, kgain = q_gain.reshape(1, dim), k_gain.reshape(1, dim)

    k_prev = shifted(k_raw, "seq", 1)
    v_prev = shifted(values, "seq", 1)

    def whole(a):
        return pl.BlockSpec(a.shape, lambda h: (0,) * a.ndim)

    qspec = pl.BlockSpec((tok, group * dim), lambda h: (0, h))
    kspec = pl.BlockSpec((tok, dim), lambda h: (0, h))
    doc_spec = pl.BlockSpec((tok, DOCS), lambda h: (0, 0))
    pair_spec = pl.BlockSpec((tok, 2 * dim), lambda h: (0, h))
    stat_spec = pl.BlockSpec((1, 8, tok), lambda h: (h, 0, 0))
    stat_shape = jax.ShapeDtypeStruct((kv_local, 8, tok), F32)
    turns = (cos, sin, cdev, sdev)
    turn_specs = [whole(a) for a in turns]
    params = pltpu.CompilerParams(vmem_limit_bytes=60 * 1024 * 1024)
    roomy = pltpu.CompilerParams(vmem_limit_bytes=57 * 1024 * 1024)
    part_spec = pl.BlockSpec((1, 8, dim), lambda h: (h, 0, 0))
    prep = [pltpu.VMEM((tok, dim), F32)] * 2 + [pltpu.VMEM((tok, DOCS), BF16)] * 2
    total = pltpu.VMEM((tok, dim), F32)

    def cost(products):
        pairs = q_local * tok * tok * 5 // 8
        return pl.CostEstimate(
            flops=2 * products * pairs * dim * 2, bytes_accessed=4 << 20, transcendentals=pairs
        )

    qh, kh, stat, kdoc, qdoc = pl.pallas_call(
        stats_kernel,
        grid=(kv_local,),
        in_specs=[qspec, kspec, kspec, qspec, whole(seg), whole(qgain), whole(kgain)] + turn_specs,
        out_specs=[qspec, kspec, stat_spec, doc_spec, doc_spec],
        out_shape=[
            jax.ShapeDtypeStruct(q_raw.shape, BF16),
            jax.ShapeDtypeStruct(k_raw.shape, BF16),
            stat_shape,
            jax.ShapeDtypeStruct((tok, DOCS), BF16),
            jax.ShapeDtypeStruct((tok, DOCS), BF16),
        ],
        scratch_shapes=prep[:2] + [pltpu.VMEM((dim + DOCS, tok), BF16), pltpu.VMEM((dim, tok), BF16)],
        compiler_params=params,
        cost_estimate=cost(2),
        name="own_statistics",
    )(q_raw, k_raw, values, grad_out, seg, qgain, kgain, *turns)

    dq_prev, back, fin, kpart_prev = pl.pallas_call(
        halo_kernel,
        grid=(kv_local,),
        in_specs=[qspec, kspec, kspec, qspec, whole(seg), doc_spec, whole(kgain)] + turn_specs + [stat_spec],
        out_specs=[qspec, pair_spec, stat_spec, part_spec],
        out_shape=[
            jax.ShapeDtypeStruct(q_raw.shape, F32),
            jax.ShapeDtypeStruct((tok, 2 * kv_local * dim), BF16),
            stat_shape,
            jax.ShapeDtypeStruct((kv_local, 8, dim), F32),
        ],
        scratch_shapes=prep[:3] + [total, total],
        compiler_params=roomy,
        cost_estimate=cost(5),
        name="previous_keys",
    )(qh, k_prev, v_prev, grad_out, seg, qdoc, kgain, *turns, stat)

    back = shifted(back, "seq", -1)

    q_grad, dy_own, dv_own, sums = pl.pallas_call(
        own_kernel,
        grid=(kv_local,),
        in_specs=[qspec, kspec, kspec, qspec, qspec, kspec, doc_spec, doc_spec, whole(qgain)]
        + turn_specs
        + [stat_spec, qspec, part_spec],
        out_specs=[qspec, kspec, kspec, pl.BlockSpec((2, dim), lambda h: (0, 0))],
        out_shape=[
            jax.ShapeDtypeStruct(q_raw.shape, BF16),
            jax.ShapeDtypeStruct(k_raw.shape, F32),
            jax.ShapeDtypeStruct(k_raw.shape, F32),
            jax.ShapeDtypeStruct((2, dim), F32),
        ],
        scratch_shapes=prep[:2] + [total, pltpu.VMEM((2, 8, dim), F32)],
        compiler_params=params,
        cost_estimate=cost(5),
        name="own_keys",
    )(qh, kh, values, grad_out, q_raw, k_raw, kdoc, qdoc, qgain, *turns, fin, dq_prev, kpart_prev)

    finish = pl.pallas_call(
        finish_kernel,
        grid=(kv_local,),
        in_specs=[kspec] * 3 + [pair_spec, whole(kgain)],
        out_specs=[kspec, kspec],
        out_shape=[jax.ShapeDtypeStruct(k_raw.shape, BF16)] * 2,
        compiler_params=roomy,
        cost_estimate=pl.CostEstimate(flops=1 << 20, bytes_accessed=5 << 20, transcendentals=0),
        name="add_returned",
    )
    for step in (("head", 1), ("head", 2), ("seq", 1)):
        sums = pairwise(sums, *step)
    sums, back = lax.optimization_barrier((sums, back))
    for step in (("seq", 2), ("seq", 4), ("seq", 8), ("seq", 16), ("head", 4)):
        sums = pairwise(sums, *step)
        if step == ("seq", 8):
            sums, (k_grad, v_grad) = lax.optimization_barrier(
                (sums, finish(k_raw, dy_own, dv_own, back, kgain))
            )
    return (q_grad, k_grad, v_grad, sums[0], sums[1])


def solution(mesh):
    in_specs = (
        P("seq", "head"),
        P("seq", "head"),
        P("seq", "head"),
        P("seq", "head"),
        P(),
        P(),
        P(),
    )
    out_specs = (P("seq", "head"), P("seq", "head"), P("seq", "head"), P(), P())
    return jax.shard_map(local, mesh=mesh, in_specs=in_specs, out_specs=out_specs, check_vma=False)
```
